32 devices in a mesh: snap: 8 (over y, x, core), clus: 4 (over z).
Axes of the slice: x: 2, y: 2, z: 4, core: 2. Of those that a mesh axis runs over, the one named last changes fastest.
Arguments:
- features: bfloat16 [32, 2048, 512], P('snap', 'clus'), parts along dimension 1, may hold values from -6 to 6
- adjacency: int32 [32, 2048, 512], P('snap', 'clus'), parts along dimension 1, may hold values 0 or 1
- first_seen: int32 [2048], P(('clus', 'snap')), parts along dimension 0, may hold values from 0 to 15
- pos_embed: bfloat16 [32, 512], replicated, may hold values from -3 to 3
- w_struct: bfloat16 [2, 512, 512], replicated, may hold values from -0.25 to 0.25
- w_query: bfloat16 [2, 512, 512], replicated, as said below
- w_key: bfloat16 [2, 512, 512], replicated, as said below
- w_value: bfloat16 [2, 512, 512], replicated, may hold values from -0.25 to 0.25
- w_out: bfloat16 [2, 512, 512], replicated, may hold values from -0.25 to 0.25
- w_up: bfloat16 [2, 512, 1024], replicated, may hold values from -0.25 to 0.25
- w_down: bfloat16 [2, 1024, 512], replicated, may hold values from -0.1875 to 0.1875
- norm_gain: float32 [2, 2, 512], replicated, may hold values from 0.1 to 1.9
Outputs:
- hidden_out: bfloat16 [32, 2048, 512], P('snap', 'clus'), parts along dimension 1
The draws below stay inside these ranges and needn't reach their ends.
There are 4 independent parts, one for each index of `clus`. The reference program is written for one: setup_inputs(seed, part) draws one part's arguments, and reference() takes and returns one part's arrays. A program takes and returns all parts, laid end to end along the dimension named above; an argument that names none is the same for every part. Nothing has to cross between parts.
Inputs may be any that keep to these rules, and one draw needn't show every extreme that they name: `w_query`: entries lie within -30 / sqrt(512) to 30 / sqrt(512). `w_key`: entries lie within -5 / sqrt(512) to 5 / sqrt(512).
All inputs are finite; a program needn't handle non-finite values. No bound on the sum of `adjacency` on one device may be relied on, other than what follows from the above.
Results may differ from the reference program's by a relative error of at most 0.012.
Values may be sent and summed in bfloat16 or wider, within the bound.
A program may use at most 128 MiB of HBM per device.

```python
import jax
import jax.numpy as jnp
from jax import lax

D = 512
FF = 1024
HEADS = 8
NODES = 512
BLOCKS = 2
S = 32


def paired_projections(key):
    base_key = jax.random.fold_in(key, 7031)
    key_part = jax.random.normal(jax.random.fold_in(base_key, 1), (BLOCKS, D, D), jnp.float32)
    noise_part = jax.random.normal(jax.random.fold_in(base_key, 2), (BLOCKS, D, D), jnp.float32)
    key_part = jnp.clip(key_part, -5.0, 5.0) * D ** (-0.5)
    noise_part = jnp.clip(noise_part, -5.0, 5.0) * D ** (-0.5)
    query_part = noise_part
    return (query_part, key_part)


def draw_w_query(key, part):
    return paired_projections(key)[0].astype(jnp.bfloat16)


def draw_w_key(key, part):
    return paired_projections(key)[1].astype(jnp.bfloat16)


def plant(entries, key, smallest, largest):
    place = [jax.random.randint(jax.random.fold_in(key, axis), (), 0, length) for axis, length in enumerate(entries.shape)]
    main_axis = entries.shape.index(max(entries.shape))
    neighbour = place[:main_axis] + [(place[main_axis] + 1) % entries.shape[main_axis]] + place[main_axis + 1:]
    return entries.at[tuple(place)].set(smallest).at[tuple(neighbour)].set(largest)


def steps_of(key, shape, split, least, largest):
    level, own = 1.0, jax.random.fold_in(key, 6)
    for axis_at, parts in split:
        steps = jnp.exp(jax.random.uniform(jax.random.fold_in(own, axis_at), (parts,), jnp.float32, least / len(split), largest / len(split)))
        level = level * jnp.repeat(steps, shape[axis_at] // parts).reshape([-1 if axis == axis_at else 1 for axis in range(len(shape))])
    return level


def bell_draw(stream_key, dims, width, most, shards=(), kind=jnp.bfloat16):
    result = width * jax.random.normal(stream_key, dims, jnp.float32)
    if shards:
        result = result * steps_of(stream_key, dims, shards, -0.22, 0.18)
    return jnp.clip(result, -most, most).astype(kind)


def setup_inputs(seed: int = 0, part: int = 0) -> dict:
    keys = jax.random.split(jax.random.key(seed), 13)
    own_keys = jax.random.split(jax.random.fold_in(keys[12], part), 13)
    return {
        "features": bell_draw(own_keys[0], (S, NODES, D), 1.0, 6.0, ((0, 8),)),
        "adjacency": plant((jax.random.randint(own_keys[1], (S, NODES, NODES), 0, 16) < 1).astype(jnp.int32), jax.random.fold_in(own_keys[1], 1), 0, 1),
        "first_seen": plant(jax.random.randint(own_keys[2], (NODES,), 0, S // 2), jax.random.fold_in(own_keys[2], 1), 0, (S // 2) - 1).astype(jnp.int32),
        "pos_embed": bell_draw(keys[3], (S, D), 0.5, 3.0),
        "w_struct": bell_draw(keys[4], (BLOCKS, D, D), D ** -0.5, 0.25),
        "w_query": draw_w_query(jax.random.fold_in(keys[12], 71), part),
        "w_key": draw_w_key(jax.random.fold_in(keys[12], 71), part),
        "w_value": bell_draw(keys[7], (BLOCKS, D, D), D ** -0.5, 0.25),
        "w_out": bell_draw(keys[8], (BLOCKS, D, D), D ** -0.5, 0.25),
        "w_up": bell_draw(keys[9], (BLOCKS, D, FF), D ** -0.5, 0.25),
        "w_down": bell_draw(keys[10], (BLOCKS, FF, D), FF ** -0.5, 0.1875),
        "norm_gain": jnp.clip(1.0 + 0.18 * jax.random.normal(keys[11], (BLOCKS, 2, D), jnp.float32), 0.1, 1.9),
    }


def layer_norm(values_in, gain):
    average = lax.optimization_barrier(jnp.mean(values_in, axis=-1, keepdims=True))
    centred = values_in - average
    scattered_rows = lax.optimization_barrier(jnp.mean(centred * centred, axis=-1, keepdims=True))
    return centred * lax.rsqrt(scattered_rows + 1e-05) * gain

def structure_output(hidden, adjacent, weight_matrix):
    degree = 1.0 + lax.optimization_barrier(jnp.sum(adjacent, axis=1)).astype(jnp.float32)
    summed = jnp.dot(adjacent.astype(jnp.bfloat16), hidden, preferred_element_type=jnp.float32) + hidden.astype(jnp.float32)
    blended_values = (summed / degree[:, None]).astype(jnp.bfloat16)
    convolved = jax.nn.elu(jnp.dot(blended_values, weight_matrix, preferred_element_type=jnp.float32))
    return (convolved + hidden.astype(jnp.float32)).astype(jnp.bfloat16)

def temporal(vertex_rows, first_seen, pos_embed, w_query, w_key, w_value, w_out, w_up, w_down, gain_pair):
    timestep_count, vertex_count, model_width = vertex_rows.shape
    head_dim = model_width // HEADS
    row_totals = vertex_rows.astype(jnp.float32) + pos_embed.astype(jnp.float32)[:, None, :]
    row_totals = row_totals.reshape(-1, model_width)
    normed = layer_norm(row_totals, gain_pair[0]).astype(jnp.bfloat16)
    shape_heads = (timestep_count, vertex_count, HEADS, head_dim)
    queries = jnp.dot(normed, w_query, preferred_element_type=jnp.float32).astype(jnp.bfloat16).reshape(shape_heads)
    key_rows = jnp.dot(normed, w_key, preferred_element_type=jnp.float32).astype(jnp.bfloat16).reshape(shape_heads)
    values = jnp.dot(normed, w_value, preferred_element_type=jnp.float32).astype(jnp.bfloat16).reshape(shape_heads)
    scores = jnp.einsum('tvhd,jvhd->vhtj', queries.astype(jnp.float32), key_rows.astype(jnp.float32)) * head_dim ** (-0.5)
    positions = jnp.arange(timestep_count, dtype=jnp.int32)
    causal = positions[None, :] <= positions[:, None]
    diagonal_mask = positions[None, :] == positions[:, None]
    present = positions[None, None, :] >= first_seen[:, None, None]
    allowed = causal[None] & (present | diagonal_mask[None])
    scores = jnp.where(allowed[:, None], scores, -1e+30)
    weights = jax.nn.softmax(scores, axis=-1).astype(jnp.bfloat16)
    attended_heads = jnp.einsum('vhtj,jvhd->tvhd', weights.astype(jnp.float32), values.astype(jnp.float32))
    attended_heads = attended_heads.astype(jnp.bfloat16).reshape(-1, model_width)
    attended = row_totals + jnp.dot(attended_heads, w_out, preferred_element_type=jnp.float32)
    normed_two = layer_norm(attended, gain_pair[1]).astype(jnp.bfloat16)
    inner_rows = jax.nn.gelu(jnp.dot(normed_two, w_up, preferred_element_type=jnp.float32)).astype(jnp.bfloat16)
    finished = attended + jnp.dot(inner_rows, w_down, preferred_element_type=jnp.float32)
    return finished.astype(jnp.bfloat16).reshape(timestep_count, vertex_count, model_width)

def reference(features, adjacency, first_seen, pos_embed, w_struct, w_query, w_key, w_value, w_out, w_up, w_down, norm_gain):
    hidden = features
    for layer in range(BLOCKS):
        weight_matrix = w_struct[layer]
        convolved = lax.map(lambda snapshot_pair: structure_output(snapshot_pair[0], snapshot_pair[1], weight_matrix), (hidden, adjacency))
        hidden = temporal(convolved, first_seen, pos_embed, w_query[layer], w_key[layer], w_value[layer], w_out[layer], w_up[layer], w_down[layer], norm_gain[layer])
    return hidden
```

```python
import functools

import jax
import jax.numpy as jnp
from jax import lax
from jax.experimental import pallas as pl
from jax.experimental.pallas import tpu as pltpu
from jax.sharding import PartitionSpec as P

HEADS = 8
LANES = 128
CHUNK = 16
GROUP = 8
F32 = jnp.float32
BF16 = jnp.bfloat16


def layer_norm(values_in, gain):
    average = jnp.mean(values_in, axis=-1, keepdims=True)
    centred = values_in - average
    scattered_rows = jnp.mean(centred * centred, axis=-1, keepdims=True)
    return centred * lax.rsqrt(scattered_rows + 1e-05) * gain


def matmul(left, right):
    return jnp.dot(left, right, preferred_element_type=F32)


def gelu(x):
    return 0.5 * x * (1.0 + jnp.tanh(0.7978845608028654 * (x + 0.044715 * (x * x * x))))


def kernel(
    n,
    features_ref,
    adjacency_ref,
    first_seen_ref,
    pos_ref,
    w_struct_ref,
    w_query_ref,
    w_key_ref,
    w_value_ref,
    w_out_ref,
    w_up_ref,
    w_down_ref,
    gain_ref,
    out_ref,
    hidden,
    adjacent,
    conv,
    arrived,
    finished,
    ws,
    wqkv,
    wo,
    wu,
    wd,
    pos,
    qkv,
    heads_out,
    in_sems,
    go_send,
    go_recv,
    back_send,
    back_recv,
    out_sem,
):
    me = lax.axis_index("snap")
    blocks = ws.shape[0]
    _, local, _, owned, width = hidden.shape
    steps = pos.shape[0]
    nodes = n * owned
    chunks = owned // CHUNK
    head_dim = width // HEADS
    rows = steps * GROUP
    groups = CHUNK // GROUP

    moves = [
        (features_ref, hidden.at[0]),
        (adjacency_ref, adjacent),
        (w_struct_ref, ws),
        (w_query_ref, wqkv.at[:, :, pl.ds(0, width)]),
        (w_key_ref, wqkv.at[:, :, pl.ds(width, width)]),
        (w_value_ref, wqkv.at[:, :, pl.ds(2 * width, width)]),
        (w_out_ref, wo),
        (w_up_ref, wu),
        (w_down_ref, wd),
    ]
    loads = [
        pltpu.make_async_copy(src, dst, in_sems.at[i]) for i, (src, dst) in enumerate(moves)
    ]
    for load in loads:
        load.start()

    barrier = pltpu.get_barrier_semaphore()

    @pl.loop(1, n)
    def _(k):
        pl.semaphore_signal(
            barrier,
            inc=1,
            device_id={"snap": lax.rem(me + k, n)},
            device_id_type=pl.DeviceIdType.MESH,
        )

    pos[...] = jnp.broadcast_to(
        pos_ref[...].astype(F32)[:, None, :], (steps, GROUP, width)
    )
    pl.semaphore_wait(barrier, n - 1)

    def go(b, c, peer, sender):
        return pltpu.make_async_remote_copy(
            src_ref=conv.at[b, c, peer],
            dst_ref=arrived.at[b, c, pl.ds(sender * local, local)],
            send_sem=go_send.at[b, c, peer],
            recv_sem=go_recv.at[b, c, sender],
            device_id={"snap": peer},
            device_id_type=pl.DeviceIdType.MESH,
        )

    def back(b, c, peer, sender):
        return pltpu.make_async_remote_copy(
            src_ref=finished.at[b, c, pl.ds(peer * local, local)],
            dst_ref=hidden.at[b + 1, :, sender, pl.ds(c * CHUNK, CHUNK)],
            send_sem=back_send.at[b, c, peer],
            recv_sem=back_recv.at[b, c, sender],
            device_id={"snap": peer},
            device_id_type=pl.DeviceIdType.MESH,
        )

    def convolve(b, c):
        mine = pl.ds(c * CHUNK, CHUNK)
        blended, own_rows = [], []
        for s in range(local):
            links = adjacent[s, :, mine, :].reshape(n * CHUNK, nodes).astype(F32)
            degree = 1.0 + jnp.sum(links, axis=-1, keepdims=True)
            own = hidden[b, s, :, mine, :].reshape(n * CHUNK, width).astype(F32)
            summed = matmul(links.astype(BF16), hidden[b, s].reshape(nodes, width)) + own
            blended.append((summed / degree).astype(BF16))
            own_rows.append(own)
        projected = matmul(jnp.concatenate(blended, axis=0), ws[b])
        projected = jnp.where(projected > 0, projected, jnp.exp(jnp.minimum(projected, 0.0)) - 1.0)
        result = (projected + jnp.concatenate(own_rows, axis=0)).astype(BF16)
        result = result.reshape(local, n, CHUNK, width)
        for s in range(local):
            conv[b, c, :, s] = result[s]

    def attend(c, g):
        base = g * rows
        lane = lax.broadcasted_iota(jnp.int32, (1, rows), 1)
        seen = jnp.zeros((1, rows), jnp.int32)
        for i in range(GROUP):
            seen = jnp.where(
                lane % GROUP == i, first_seen_ref[c * CHUNK + g * GROUP + i], seen
            )
        row_at = lax.broadcasted_iota(jnp.int32, (rows, rows), 0)
        col_at = lax.broadcasted_iota(jnp.int32, (rows, rows), 1)
        t, j = row_at // GROUP, col_at // GROUP
        allowed = (row_at % GROUP == col_at % GROUP) & (j <= t) & ((j >= seen) | (j == t))
        bias = jnp.where(allowed, 0.0, -1e30)
        tile_lane = lax.broadcasted_iota(jnp.int32, (1, LANES), 1)
        for tile in range(width // LANES):
            q = qkv[pl.ds(base, rows), pl.ds(tile * LANES, LANES)]
            k = qkv[pl.ds(base, rows), pl.ds(width + tile * LANES, LANES)]
            v = qkv[pl.ds(base, rows), pl.ds(2 * width + tile * LANES, LANES)]
            total = jnp.zeros((rows, 2 * LANES), F32)
            for h in range(LANES // head_dim):
                chosen = jnp.where(tile_lane // head_dim == h, 1.0, 0.0).astype(BF16)
                scores = lax.dot_general(
                    q, k * chosen, (((1,), (1,)), ((), ())), preferred_element_type=F32
                )
                scores = scores + bias
                top = jnp.max(scores, axis=-1, keepdims=True)
                weights = jnp.exp(scores - top).astype(BF16)
                wide = jnp.concatenate(
                    [v * chosen, jnp.broadcast_to(chosen, (rows, LANES))], axis=1
                )
                total = total + matmul(weights, wide)
            heads_out[pl.ds(base, rows), pl.ds(tile * LANES, LANES)] = (
                total[:, :LANES] / total[:, LANES:]
            ).astype(BF16)

    def temporal(b, c):
        arrivals = arrived[b, c].astype(F32)
        summed = jnp.concatenate(
            [
                (arrivals[:, g * GROUP : (g + 1) * GROUP, :] + pos[...]).reshape(rows, width)
                for g in range(groups)
            ],
            axis=0,
        )
        normed = layer_norm(summed, gain_ref[b, pl.ds(0, 1), :]).astype(BF16)
        qkv[:, pl.ds(0, width)] = (
            matmul(normed, wqkv[b, :, pl.ds(0, width)]) * head_dim ** (-0.5)
        ).astype(BF16)
        qkv[:, pl.ds(width, 2 * width)] = matmul(
            normed, wqkv[b, :, pl.ds(width, 2 * width)]
        ).astype(BF16)
        for g in range(groups):
            attend(c, g)
        attended = summed + matmul(heads_out[...], wo[b])
        normed_two = layer_norm(attended, gain_ref[b, pl.ds(1, 1), :]).astype(BF16)
        inner = gelu(matmul(normed_two, wu[b])).astype(BF16)
        result = attended + matmul(inner, wd[b])
        finished[b, c] = jnp.concatenate(
            [
                result[g * rows : (g + 1) * rows].reshape(steps, GROUP, width)
                for g in range(groups)
            ],
            axis=1,
        ).astype(BF16)

    for load in loads:
        load.wait()

    @pl.loop(0, blocks)
    def _(b):
        @pl.loop(0, chunks)
        def _(c):
            convolve(b, c)

            @pl.loop(1, n)
            def _(k):
                go(b, c, lax.rem(me + k, n), me).start()

            arrived[b, c, pl.ds(me * local, local)] = conv[b, c, me]

        @pl.loop(0, chunks)
        def _(c):
            @pl.loop(1, n)
            def _(k):
                peer = lax.rem(me + k, n)
                go(b, c, peer, peer).wait_recv()

            temporal(b, c)

            @pl.loop(1, n)
            def _(k):
                back(b, c, lax.rem(me + k, n), me).start()

            hidden[b + 1, :, me, pl.ds(c * CHUNK, CHUNK), :] = finished[
                b, c, pl.ds(me * local, local)
            ]

        @pl.loop(0, chunks)
        def _(c):
            @pl.loop(1, n)
            def _(k):
                peer = lax.rem(me + k, n)
                back(b, c, peer, peer).wait_recv()

    store = pltpu.make_async_copy(hidden.at[blocks], out_ref, out_sem)
    store.start()

    @pl.loop(0, blocks)
    def _(b):
        @pl.loop(0, chunks)
        def _(c):
            @pl.loop(1, n)
            def _(k):
                peer = lax.rem(me + k, n)
                go(b, c, peer, me).wait_send()
                back(b, c, peer, me).wait_send()

    store.wait()


def on_device(n, features, adjacency, first_seen, pos_embed, *weights):
    local, nodes, width = features.shape
    blocks, _, hidden_units = weights[5].shape
    owned = nodes // n
    chunks = owned // CHUNK
    steps = pos_embed.shape[0]
    chunk_rows = steps * CHUNK
    anywhere = pl.BlockSpec(memory_space=pl.ANY)
    in_vmem = pl.BlockSpec(memory_space=pltpu.VMEM)
    result = pl.pallas_call(
        functools.partial(kernel, n),
        out_shape=jax.ShapeDtypeStruct((local, n, owned, width), BF16),
        in_specs=[
            anywhere,
            anywhere,
            pl.BlockSpec(memory_space=pltpu.SMEM),
            in_vmem,
            *[anywhere] * 7,
            in_vmem,
        ],
        out_specs=anywhere,
        scratch_shapes=[
            pltpu.VMEM((blocks + 1, local, n, owned, width), BF16),
            pltpu.VMEM((local, n, owned, nodes), jnp.int32),
            pltpu.VMEM((blocks, chunks, n, local, CHUNK, width), BF16),
            pltpu.VMEM((blocks, chunks, steps, CHUNK, width), BF16),
            pltpu.VMEM((blocks, chunks, steps, CHUNK, width), BF16),
            pltpu.VMEM((blocks, width, width), BF16),
            pltpu.VMEM((blocks, width, 3 * width), BF16),
            pltpu.VMEM((blocks, width, width), BF16),
            pltpu.VMEM((blocks, width, hidden_units), BF16),
            pltpu.VMEM((blocks, hidden_units, width), BF16),
            pltpu.VMEM((steps, GROUP, width), F32),
            pltpu.VMEM((chunk_rows, 3 * width), BF16),
            pltpu.VMEM((chunk_rows, width), BF16),
            pltpu.SemaphoreType.DMA((9,)),
            pltpu.SemaphoreType.DMA((blocks, chunks, n)),
            pltpu.SemaphoreType.DMA((blocks, chunks, n)),
            pltpu.SemaphoreType.DMA((blocks, chunks, n)),
            pltpu.SemaphoreType.DMA((blocks, chunks, n)),
            pltpu.SemaphoreType.DMA,
        ],
        compiler_params=pltpu.CompilerParams(
            collective_id=0, has_side_effects=True, vmem_limit_bytes=56 * 2**20
        ),
    )(
        features.reshape(local, n, owned, width),
        adjacency.reshape(local, n, owned, nodes),
        first_seen,
        pos_embed,
        *weights,
    )
    return result.reshape(local, nodes, width)


def solution(mesh):
    in_specs = (
        P("snap", "clus", None),
        P("snap", "clus", None),
        P(("clus", "snap")),
        *[P()] * 9,
    )
    return jax.shard_map(
        functools.partial(on_device, mesh.shape["snap"]),
        mesh=mesh,
        in_specs=in_specs,
        out_specs=P("snap", "clus", None),
        check_vma=False,
    )
```

```python
import functools

import jax
import jax.numpy as jnp
from jax import lax
from jax.experimental import pallas as pl
from jax.experimental.pallas import tpu as pltpu
from jax.sharding import PartitionSpec as P

HEADS = 8
LANES = 128
CHUNK = 16
GROUP = 8
SPANS = 2
F32 = jnp.float32
BF16 = jnp.bfloat16


def layer_norm(values_in, gain):
    average = jnp.mean(values_in, axis=-1, keepdims=True)
    centred = values_in - average
    scattered_rows = jnp.mean(centred * centred, axis=-1, keepdims=True)
    return centred * lax.rsqrt(scattered_rows + 1e-05) * gain


def matmul(left, right):
    return jnp.dot(left, right, preferred_element_type=F32)


def gelu(x):
    half = 0.5 * x
    return half + half * jnp.tanh(x * (0.7978845608028654 + 0.035677408136300125 * (x * x)))


def kernel(
    n,
    features_ref,
    adjacency_ref,
    first_seen_ref,
    pos_ref,
    w_struct_ref,
    w_query_ref,
    w_key_ref,
    w_value_ref,
    w_out_ref,
    w_up_ref,
    w_down_ref,
    gain_ref,
    out_ref,
    hidden,
    adjacent,
    conv,
    arrived,
    finished,
    ws,
    wqkv,
    wo,
    wu,
    wd,
    pos,
    qkv,
    heads_out,
    in_sems,
    link_sems,
    go_send,
    go_recv,
    back_send,
    back_recv,
    out_sem,
):
    me = lax.axis_index("snap")
    blocks = ws.shape[0]
    _, local, _, owned, width = hidden.shape
    steps = pos.shape[0]
    nodes = n * owned
    chunks = owned // CHUNK
    head_dim = width // HEADS
    rows = steps * GROUP
    groups = CHUNK // GROUP

    def load_links(c):
        part = pl.ds(c * CHUNK, CHUNK)
        return pltpu.make_async_copy(
            adjacency_ref.at[:, :, part], adjacent.at[:, :, part], link_sems.at[c]
        )

    moves = [
        (features_ref, hidden.at[0]),
        (w_struct_ref, ws),
        (w_query_ref, wqkv.at[:, :, pl.ds(0, width)]),
        (w_key_ref, wqkv.at[:, :, pl.ds(width, width)]),
        (w_value_ref, wqkv.at[:, :, pl.ds(2 * width, width)]),
        (w_out_ref, wo),
        (w_up_ref, wu),
        (w_down_ref, wd),
    ]
    loads = [
        pltpu.make_async_copy(src, dst, in_sems.at[i]) for i, (src, dst) in enumerate(moves)
    ]
    loads[0].start()
    load_links(0).start()
    loads[1].start()
    for c in range(1, chunks):
        load_links(c).start()
    for load in loads[2:]:
        load.start()

    barrier = pltpu.get_barrier_semaphore()
    for k in range(1, n):
        pl.semaphore_signal(
            barrier,
            inc=1,
            device_id={"snap": lax.rem(me + k, n)},
            device_id_type=pl.DeviceIdType.MESH,
        )
    pos[...] = jnp.broadcast_to(
        pos_ref[...].astype(F32)[:, None, :], (steps, GROUP, width)
    )

    def send(src, dst, send_sem, recv_sem, peer):
        return pltpu.make_async_remote_copy(
            src_ref=src,
            dst_ref=dst,
            send_sem=send_sem,
            recv_sem=recv_sem,
            device_id={"snap": peer},
            device_id_type=pl.DeviceIdType.MESH,
        )

    others = pl.ds(0, n - 1)

    def go(b, c, peer):
        return send(
            conv.at[b, c, peer],
            arrived.at[b, c, pl.ds(me * local, local)],
            go_send.at[b],
            go_recv.at[b, c],
            peer,
        )

    def back(b, c, peer, target):
        return send(
            finished.at[b, c, pl.ds(peer * local, local)],
            target.at[:, me, pl.ds(c * CHUNK, CHUNK)],
            back_send.at[b],
            back_recv.at[b],
            peer,
        )

    def await_chunk(b, c):
        view = arrived.at[b, c, pl.ds(0, (n - 1) * local)]
        send(view, view, go_send.at[b], go_recv.at[b, c], me).wait_recv()

    def await_back(b, target):
        view = target.at[:, others]
        send(view, view, back_send.at[b], back_recv.at[b], me).wait_recv()

    def await_sent(b):
        view = conv.at[b, :, others]
        send(view, view, go_send.at[b], go_recv.at[b, 0], me).wait_send()
        view = finished.at[b, :, pl.ds(0, (n - 1) * local)]
        send(view, view, back_send.at[b], back_recv.at[b], me).wait_send()

    def convolve(b, c):
        mine = pl.ds(c * CHUNK, CHUNK)
        blended, own_rows = [], []
        for s in range(local):
            links = adjacent[s, :, mine, :].reshape(n * CHUNK, nodes).astype(F32)
            degree = 1.0 + jnp.sum(links, axis=-1, keepdims=True)
            own = hidden[b, s, :, mine, :].reshape(n * CHUNK, width).astype(F32)
            summed = matmul(links.astype(BF16), hidden[b, s].reshape(nodes, width)) + own
            blended.append((summed * (1.0 / degree)).astype(BF16))
            own_rows.append(own)
        projected = matmul(jnp.concatenate(blended, axis=0), ws[b])
        projected = jnp.where(projected > 0, projected, jnp.exp(jnp.minimum(projected, 0.0)) - 1.0)
        result = (projected + jnp.concatenate(own_rows, axis=0)).astype(BF16)
        result = result.reshape(local, n, CHUNK, width)
        for s in range(local):
            conv[b, c, :, s] = result[s]

    def attend(c, g):
        base = g * rows
        lane = lax.broadcasted_iota(jnp.int32, (1, rows), 1)
        seen = jnp.zeros((1, rows), jnp.int32)
        for i in range(GROUP):
            seen = jnp.where(
                lane % GROUP == i, first_seen_ref[c * CHUNK + g * GROUP + i], seen
            )
        row_at = lax.broadcasted_iota(jnp.int32, (rows, rows), 0)
        col_at = lax.broadcasted_iota(jnp.int32, (rows, rows), 1)
        t, j = row_at // GROUP, col_at // GROUP
        allowed = (row_at % GROUP == col_at % GROUP) & (j <= t) & ((j >= seen) | (j == t))
        bias = jnp.where(allowed, 0.0, -1e30)
        tile_lane = lax.broadcasted_iota(jnp.int32, (1, LANES), 1)
        for tile in range(width // LANES):
            q = qkv[pl.ds(base, rows), pl.ds(tile * LANES, LANES)]
            k = qkv[pl.ds(base, rows), pl.ds(width + tile * LANES, LANES)]
            v = qkv[pl.ds(base, rows), pl.ds(2 * width + tile * LANES, LANES)]
            totals = [None] * SPANS
            for h in range(LANES // head_dim):
                chosen = jnp.where(tile_lane // head_dim == h, 1.0, 0.0).astype(BF16)
                keys = k * chosen
                wide = jnp.concatenate(
                    [v * chosen, jnp.broadcast_to(chosen, (rows, LANES))], axis=1
                )
                for i in range(SPANS):
                    start, end = i * (rows // SPANS), (i + 1) * (rows // SPANS)
                    scores = lax.dot_general(
                        q[start:end],
                        keys[:end],
                        (((1,), (1,)), ((), ())),
                        preferred_element_type=F32,
                    )
                    scores = scores + bias[start:end, :end]
                    top = jnp.max(scores, axis=-1, keepdims=True)
                    weights = jnp.exp(scores - top).astype(BF16)
                    part = matmul(weights, wide[:end])
                    totals[i] = part if h == 0 else totals[i] + part
            for i, total in enumerate(totals):
                heads_out[
                    pl.ds(base + i * (rows // SPANS), rows // SPANS), pl.ds(tile * LANES, LANES)
                ] = (total[:, :LANES] / total[:, LANES:]).astype(BF16)

    def temporal(b, c):
        arrivals = arrived[b, c].astype(F32)
        summed = jnp.concatenate(
            [
                (arrivals[:, g * GROUP : (g + 1) * GROUP, :] + pos[...]).reshape(rows, width)
                for g in range(groups)
            ],
            axis=0,
        )
        normed = layer_norm(summed, gain_ref[b, pl.ds(0, 1), :]).astype(BF16)
        qkv[:, pl.ds(0, width)] = (
            matmul(normed, wqkv[b, :, pl.ds(0, width)]) * head_dim ** (-0.5)
        ).astype(BF16)
        qkv[:, pl.ds(width, 2 * width)] = matmul(
            normed, wqkv[b, :, pl.ds(width, 2 * width)]
        ).astype(BF16)
        for g in range(groups):
            attend(c, g)
        attended = summed + matmul(heads_out[...], wo[b])
        normed_two = layer_norm(attended, gain_ref[b, pl.ds(1, 1), :]).astype(BF16)
        inner = gelu(matmul(normed_two, wu[b])).astype(BF16)
        result = attended + matmul(inner, wd[b])
        finished[b, c] = jnp.concatenate(
            [
                result[g * rows : (g + 1) * rows].reshape(steps, GROUP, width)
                for g in range(groups)
            ],
            axis=1,
        ).astype(BF16)

    last = blocks - 1
    peers = [lax.rem(me + k, n) for k in range(1, n)]
    loads[0].wait()
    loads[1].wait()

    @pl.loop(0, blocks)
    def _(b):
        @pl.loop(0, chunks)
        def _(c):
            @pl.when(b == 0)
            def _():
                load_links(c).wait()

            convolve(b, c)

            @pl.when((b == 0) & (c == 0))
            def _():
                pl.semaphore_wait(barrier, n - 1)

            for peer in peers:
                go(b, c, peer).start()
            arrived[b, c, pl.ds(me * local, local)] = conv[b, c, me]

        @pl.when(b == 0)
        def _():
            for load in loads[2:]:
                load.wait()

        @pl.loop(0, chunks)
        def _(c):
            await_chunk(b, c)
            temporal(b, c)
            part = pl.ds(c * CHUNK, CHUNK)
            own = pl.ds(me * local, local)

            @pl.when(b < last)
            def _():
                for peer in peers:
                    back(b, c, peer, hidden.at[b + 1]).start()
                hidden[b + 1, :, me, part, :] = finished[b, c, own]

            @pl.when(b == last)
            def _():
                for peer in peers:
                    back(b, c, peer, out_ref).start()
                pltpu.make_async_copy(
                    finished.at[b, c, own], out_ref.at[:, me, part], out_sem
                ).start()

        @pl.when(b < last)
        def _():
            await_back(b, hidden.at[b + 1])

    for b in range(blocks):
        await_sent(b)
    await_back(last, out_ref)
    pltpu.make_async_copy(
        finished.at[last, :, pl.ds(0, local)], finished.at[last, :, pl.ds(0, local)], out_sem
    ).wait()


def on_device(n, features, adjacency, first_seen, pos_embed, *weights):
    local, nodes, width = features.shape
    blocks, _, hidden_units = weights[5].shape
    owned = nodes // n
    chunks = owned // CHUNK
    steps = pos_embed.shape[0]
    chunk_rows = steps * CHUNK
    anywhere = pl.BlockSpec(memory_space=pl.ANY)
    in_vmem = pl.BlockSpec(memory_space=pltpu.VMEM)
    result = pl.pallas_call(
        functools.partial(kernel, n),
        out_shape=jax.ShapeDtypeStruct((local, n, owned, width), BF16),
        in_specs=[
            anywhere,
            anywhere,
            pl.BlockSpec(memory_space=pltpu.SMEM),
            in_vmem,
            *[anywhere] * 7,
            in_vmem,
        ],
        out_specs=anywhere,
        scratch_shapes=[
            pltpu.VMEM((blocks, local, n, owned, width), BF16),
            pltpu.VMEM((local, n, owned, nodes), jnp.int32),
            pltpu.VMEM((blocks, chunks, n, local, CHUNK, width), BF16),
            pltpu.VMEM((blocks, chunks, steps, CHUNK, width), BF16),
            pltpu.VMEM((blocks, chunks, steps, CHUNK, width), BF16),
            pltpu.VMEM((blocks, width, width), BF16),
            pltpu.VMEM((blocks, width, 3 * width), BF16),
            pltpu.VMEM((blocks, width, width), BF16),
            pltpu.VMEM((blocks, width, hidden_units), BF16),
            pltpu.VMEM((blocks, hidden_units, width), BF16),
            pltpu.VMEM((steps, GROUP, width), F32),
            pltpu.VMEM((chunk_rows, 3 * width), BF16),
            pltpu.VMEM((chunk_rows, width), BF16),
            pltpu.SemaphoreType.DMA((8,)),
            pltpu.SemaphoreType.DMA((chunks,)),
            pltpu.SemaphoreType.DMA((blocks,)),
            pltpu.SemaphoreType.DMA((blocks, chunks)),
            pltpu.SemaphoreType.DMA((blocks,)),
            pltpu.SemaphoreType.DMA((blocks,)),
            pltpu.SemaphoreType.DMA,
        ],
        compiler_params=pltpu.CompilerParams(
            collective_id=0, has_side_effects=True, vmem_limit_bytes=56 * 2**20
        ),
    )(
        features.reshape(local, n, owned, width),
        adjacency.reshape(local, n, owned, nodes),
        first_seen,
        pos_embed,
        *weights,
    )
    return result.reshape(local, nodes, width)


def solution(mesh):
    in_specs = (
        P("snap", "clus", None),
        P("snap", "clus", None),
        P(("clus", "snap")),
        *[P()] * 9,
    )
    return jax.shard_map(
        functools.partial(on_device, mesh.shape["snap"]),
        mesh=mesh,
        in_specs=in_specs,
        out_specs=P("snap", "clus", None),
        check_vma=False,
    )
```

```python
import functools

import jax
import jax.numpy as jnp
from jax import lax
from jax.experimental import pallas as pl
from jax.experimental.pallas import tpu as pltpu
from jax.sharding import PartitionSpec as P

HEADS = 8
LANES = 128
CHUNK = 16
GROUP = 8
SPANS = 2
LAG = 4
FF_TILE = 256
F32 = jnp.float32
BF16 = jnp.bfloat16


def layer_norm(values_in, gain):
    average = jnp.mean(values_in, axis=-1, keepdims=True)
    centred = values_in - average
    scattered_rows = jnp.mean(centred * centred, axis=-1, keepdims=True)
    return centred * lax.rsqrt(scattered_rows + 1e-05) * gain


def matmul(left, right):
    return jnp.dot(left, right, preferred_element_type=F32)


def gelu(x):
    half = 0.5 * x
    return half + half * jnp.tanh(x * (0.7978845608028654 + 0.035677408136300125 * (x * x)))


def kernel(
    n,
    features_ref,
    adjacency_ref,
    first_seen_ref,
    pos_ref,
    w_struct_ref,
    w_query_ref,
    w_key_ref,
    w_value_ref,
    w_out_ref,
    w_up_ref,
    w_down_ref,
    gain_ref,
    out_ref,
    hidden,
    adjacent,
    conv,
    arrived,
    finished,
    ws,
    wqkv,
    wo,
    wu,
    wd,
    pos,
    qkv,
    heads_out,
    bias,
    inner,
    in_sems,
    link_sems,
    go_send,
    go_recv,
    back_send,
    back_recv,
    out_sem,
):
    me = lax.axis_index("snap")
    blocks = ws.shape[0]
    _, local, _, owned, width = hidden.shape
    steps = pos.shape[0]
    nodes = n * owned
    chunks = owned // CHUNK
    head_dim = width // HEADS
    rows = steps * GROUP
    groups = CHUNK // GROUP

    def load_links(c):
        part = pl.ds(c * CHUNK, CHUNK)
        return pltpu.make_async_copy(
            adjacency_ref.at[:, :, part], adjacent.at[:, :, part], link_sems.at[c]
        )

    moves = [
        (features_ref, hidden.at[0]),
        (w_struct_ref, ws),
        (w_query_ref, wqkv.at[:, :, pl.ds(0, width)]),
        (w_key_ref, wqkv.at[:, :, pl.ds(width, width)]),
        (w_value_ref, wqkv.at[:, :, pl.ds(2 * width, width)]),
        (w_out_ref, wo),
        (w_up_ref, wu),
        (w_down_ref, wd),
    ]
    loads = [
        pltpu.make_async_copy(src, dst, in_sems.at[i]) for i, (src, dst) in enumerate(moves)
    ]
    loads[0].start()
    load_links(0).start()
    loads[1].start()
    for c in range(1, chunks):
        load_links(c).start()
    for load in loads[2:]:
        load.start()

    barrier = pltpu.get_barrier_semaphore()
    for k in range(1, n):
        pl.semaphore_signal(
            barrier,
            inc=1,
            device_id={"snap": lax.rem(me + k, n)},
            device_id_type=pl.DeviceIdType.MESH,
        )
    pos[...] = jnp.broadcast_to(
        pos_ref[...].astype(F32)[:, None, :], (steps, GROUP, width)
    )

    def send(src, dst, send_sem, recv_sem, peer):
        return pltpu.make_async_remote_copy(
            src_ref=src,
            dst_ref=dst,
            send_sem=send_sem,
            recv_sem=recv_sem,
            device_id={"snap": peer},
            device_id_type=pl.DeviceIdType.MESH,
        )

    others = pl.ds(0, n - 1)

    def go(b, c, peer):
        return send(
            conv.at[b, c, peer],
            arrived.at[b, c, pl.ds(me * local, local)],
            go_send.at[b],
            go_recv.at[b, c],
            peer,
        )

    def back(b, c, peer, target):
        return send(
            finished.at[b, c, pl.ds(peer * local, local)],
            target.at[:, me, pl.ds(c * CHUNK, CHUNK)],
            back_send.at[b],
            back_recv.at[b],
            peer,
        )

    def await_chunk(b, c):
        view = arrived.at[b, c, pl.ds(0, (n - 1) * local)]
        send(view, view, go_send.at[b], go_recv.at[b, c], me).wait_recv()

    def await_back(b, target):
        view = target.at[:, others]
        send(view, view, back_send.at[b], back_recv.at[b], me).wait_recv()

    def await_sent(b):
        view = conv.at[b, :, others]
        send(view, view, go_send.at[b], go_recv.at[b, 0], me).wait_send()
        view = finished.at[b, :, pl.ds(0, (n - 1) * local)]
        send(view, view, back_send.at[b], back_recv.at[b], me).wait_send()

    def convolve(b, c):
        mine = pl.ds(c * CHUNK, CHUNK)
        blended, own_rows = [], []
        for s in range(local):
            links = adjacent[s, :, mine, :].reshape(n * CHUNK, nodes).astype(F32)
            degree = 1.0 + jnp.sum(links, axis=-1, keepdims=True)
            own = hidden[b, s, :, mine, :].reshape(n * CHUNK, width).astype(F32)
            summed = matmul(links.astype(BF16), hidden[b, s].reshape(nodes, width)) + own
            blended.append((summed * (1.0 / degree)).astype(BF16))
            own_rows.append(own)
        projected = matmul(jnp.concatenate(blended, axis=0), ws[b])
        projected = jnp.where(projected > 0, projected, jnp.exp(jnp.minimum(projected, 0.0)) - 1.0)
        result = (projected + jnp.concatenate(own_rows, axis=0)).astype(BF16)
        result = result.reshape(local, n, CHUNK, width)
        for s in range(local):
            conv[b, c, :, s] = result[s]

    def mask_of(c, g):
        lane = lax.broadcasted_iota(jnp.int32, (1, rows), 1)
        seen = jnp.zeros((1, rows), jnp.int32)
        for i in range(GROUP):
            seen = jnp.where(
                lane % GROUP == i, first_seen_ref[c * CHUNK + g * GROUP + i], seen
            )
        row_at = lax.broadcasted_iota(jnp.int32, (rows, rows), 0)
        col_at = lax.broadcasted_iota(jnp.int32, (rows, rows), 1)
        t, j = row_at // GROUP, col_at // GROUP
        allowed = (row_at % GROUP == col_at % GROUP) & (j <= t) & ((j >= seen) | (j == t))
        bias[g] = jnp.where(allowed, 0.0, -1e30)

    def attend(g, tile):
        at = g * rows
        span = rows // SPANS
        tile_lane = lax.broadcasted_iota(jnp.int32, (1, LANES), 1)
        q = qkv[at : at + rows, tile * LANES : (tile + 1) * LANES]
        k = qkv[at : at + rows, width + tile * LANES : width + (tile + 1) * LANES]
        v = qkv[at : at + rows, 2 * width + tile * LANES : 2 * width + (tile + 1) * LANES]
        totals = [None] * SPANS
        for h in range(LANES // head_dim):
            chosen = jnp.where(tile_lane // head_dim == h, 1.0, 0.0).astype(BF16)
            keys = k * chosen
            wide = jnp.concatenate(
                [v * chosen, jnp.broadcast_to(chosen, (rows, LANES))], axis=1
            )
            for i in range(SPANS):
                start, end = i * span, (i + 1) * span
                scores = lax.dot_general(
                    q[start:end],
                    keys[:end],
                    (((1,), (1,)), ((), ())),
                    preferred_element_type=F32,
                )
                scores = scores + bias[g, start:end, :end]
                top = jnp.max(scores, axis=-1, keepdims=True)
                weights = jnp.exp(scores - top).astype(BF16)
                part = matmul(weights, wide[:end])
                totals[i] = part if h == 0 else totals[i] + part
        for i, total in enumerate(totals):
            heads_out[
                at + i * span : at + (i + 1) * span, tile * LANES : (tile + 1) * LANES
            ] = (total[:, :LANES] / total[:, LANES:]).astype(BF16)

    def group_steps(b, c, g, results):
        at = slice(g * rows, (g + 1) * rows)
        arrivals = arrived[b, c].astype(F32)[:, g * GROUP : (g + 1) * GROUP, :]
        summed = (arrivals + pos[...]).reshape(rows, width)
        normed = layer_norm(summed, gain_ref[b, pl.ds(0, 1), :]).astype(BF16)
        mask_of(c, g)
        yield
        qkv[at, :width] = (matmul(normed, wqkv[b, :, :width]) * head_dim ** (-0.5)).astype(BF16)
        yield
        qkv[at, width : 2 * width] = matmul(normed, wqkv[b, :, width : 2 * width]).astype(BF16)
        yield
        qkv[at, 2 * width :] = matmul(normed, wqkv[b, :, 2 * width :]).astype(BF16)
        yield
        for tile in range(width // LANES):
            attend(g, tile)
            yield
        attended = summed + matmul(heads_out[at, :], wo[b])
        normed_two = layer_norm(attended, gain_ref[b, pl.ds(1, 1), :]).astype(BF16)
        yield
        hidden_units = wu.shape[2]
        for start in range(0, hidden_units, FF_TILE):
            part = slice(start, start + FF_TILE)
            inner[at, part] = gelu(matmul(normed_two, wu[b, :, part])).astype(BF16)
            yield
        results[g] = (attended + matmul(inner[at, :], wd[b])).reshape(steps, GROUP, width)

    def temporal(b, c):
        results = [None] * groups
        waiting = [group_steps(b, c, g, results) for g in range(groups)]
        running, tick = [], 0
        while waiting or running:
            if waiting and tick % LAG == 0:
                running.append(waiting.pop(0))
            for steps_left in list(running):
                if next(steps_left, 0) == 0:
                    running.remove(steps_left)
            tick += 1
        finished[b, c] = jnp.concatenate(results, axis=1).astype(BF16)

    last = blocks - 1
    peers = [lax.rem(me + k, n) for k in range(1, n)]
    loads[0].wait()
    loads[1].wait()

    @pl.loop(0, blocks)
    def _(b):
        @pl.loop(0, chunks)
        def _(c):
            @pl.when(b == 0)
            def _():
                load_links(c).wait()

            convolve(b, c)

            @pl.when((b == 0) & (c == 0))
            def _():
                pl.semaphore_wait(barrier, n - 1)

            for peer in peers:
                go(b, c, peer).start()
            arrived[b, c, pl.ds(me * local, local)] = conv[b, c, me]

        @pl.when(b == 0)
        def _():
            for load in loads[2:]:
                load.wait()

        @pl.loop(0, chunks)
        def _(c):
            await_chunk(b, c)
            temporal(b, c)
            part = pl.ds(c * CHUNK, CHUNK)
            own = pl.ds(me * local, local)

            @pl.when(b < last)
            def _():
                for peer in peers:
                    back(b, c, peer, hidden.at[b + 1]).start()
                hidden[b + 1, :, me, part, :] = finished[b, c, own]

            @pl.when(b == last)
            def _():
                for peer in peers:
                    back(b, c, peer, out_ref).start()
                pltpu.make_async_copy(
                    finished.at[b, c, own], out_ref.at[:, me, part], out_sem
                ).start()

        @pl.when(b < last)
        def _():
            await_back(b, hidden.at[b + 1])

    for b in range(blocks):
        await_sent(b)
    await_back(last, out_ref)
    pltpu.make_async_copy(
        finished.at[last, :, pl.ds(0, local)], finished.at[last, :, pl.ds(0, local)], out_sem
    ).wait()


def on_device(n, features, adjacency, first_seen, pos_embed, *weights):
    local, nodes, width = features.shape
    blocks, _, hidden_units = weights[5].shape
    owned = nodes // n
    chunks = owned // CHUNK
    steps = pos_embed.shape[0]
    chunk_rows = steps * CHUNK
    anywhere = pl.BlockSpec(memory_space=pl.ANY)
    in_vmem = pl.BlockSpec(memory_space=pltpu.VMEM)
    result = pl.pallas_call(
        functools.partial(kernel, n),
        out_shape=jax.ShapeDtypeStruct((local, n, owned, width), BF16),
        in_specs=[
            anywhere,
            anywhere,
            pl.BlockSpec(memory_space=pltpu.SMEM),
            in_vmem,
            *[anywhere] * 7,
            in_vmem,
        ],
        out_specs=anywhere,
        scratch_shapes=[
            pltpu.VMEM((blocks, local, n, owned, width), BF16),
            pltpu.VMEM((local, n, owned, nodes), jnp.int32),
            pltpu.VMEM((blocks, chunks, n, local, CHUNK, width), BF16),
            pltpu.VMEM((blocks, chunks, steps, CHUNK, width), BF16),
            pltpu.VMEM((blocks, chunks, steps, CHUNK, width), BF16),
            pltpu.VMEM((blocks, width, width), BF16),
            pltpu.VMEM((blocks, width, 3 * width), BF16),
            pltpu.VMEM((blocks, width, width), BF16),
            pltpu.VMEM((blocks, width, hidden_units), BF16),
            pltpu.VMEM((blocks, hidden_units, width), BF16),
            pltpu.VMEM((steps, GROUP, width), F32),
            pltpu.VMEM((chunk_rows, 3 * width), BF16),
            pltpu.VMEM((chunk_rows, width), BF16),
            pltpu.VMEM((CHUNK // GROUP, steps * GROUP, steps * GROUP), F32),
            pltpu.VMEM((chunk_rows, hidden_units), BF16),
            pltpu.SemaphoreType.DMA((8,)),
            pltpu.SemaphoreType.DMA((chunks,)),
            pltpu.SemaphoreType.DMA((blocks,)),
            pltpu.SemaphoreType.DMA((blocks, chunks)),
            pltpu.SemaphoreType.DMA((blocks,)),
            pltpu.SemaphoreType.DMA((blocks,)),
            pltpu.SemaphoreType.DMA,
        ],
        compiler_params=pltpu.CompilerParams(
            collective_id=0, has_side_effects=True, vmem_limit_bytes=56 * 2**20
        ),
    )(
        features.reshape(local, n, owned, width),
        adjacency.reshape(local, n, owned, nodes),
        first_seen,
        pos_embed,
        *weights,
    )
    return result.reshape(local, nodes, width)


def solution(mesh):
    in_specs = (
        P("snap", "clus", None),
        P("snap", "clus", None),
        P(("clus", "snap")),
        *[P()] * 9,
    )
    return jax.shard_map(
        functools.partial(on_device, mesh.shape["snap"]),
        mesh=mesh,
        in_specs=in_specs,
        out_specs=P("snap", "clus", None),
        check_vma=False,
    )
```

```python
import functools

import jax
import jax.numpy as jnp
from jax import lax
from jax.experimental import pallas as pl
from jax.experimental.pallas import tpu as pltpu
from jax.sharding import PartitionSpec as P

HEADS = 8
LANES = 128
CHUNK = 16
GROUP = 8
SPANS = 2
LAG = 4
FF_TILE = 256
F32 = jnp.float32
BF16 = jnp.bfloat16


def layer_norm(values_in, gain):
    average = jnp.mean(values_in, axis=-1, keepdims=True)
    centred = values_in - average
    scattered_rows = jnp.mean(centred * centred, axis=-1, keepdims=True)
    return centred * lax.rsqrt(scattered_rows + 1e-05) * gain


def matmul(left, right):
    return jnp.dot(left, right, preferred_element_type=F32)


def gelu(x):
    half = 0.5 * x
    return half + half * jnp.tanh(x * (0.7978845608028654 + 0.035677408136300125 * (x * x)))


def peers_of(me, n):
    bits = n.bit_length() - 1
    if 2**bits != n or bits < 3:
        return [lax.rem(me + k, n) for k in range(1, n)]
    digits = [(me // 2**i) % 2 for i in range(bits)]
    core = digits[0]
    order = sorted(range(1, n), key=lambda m: (m < 2, bin(m // 2).count("1"), m))
    peers = []
    for m in order:
        flips = [(m // 2**i) % 2 for i in range(bits)]
        low, high = flips[1], flips[2]
        flips[1] = low * (1 - core) + high * core
        flips[2] = high * (1 - core) + low * core
        peers.append(sum(((d + f) % 2) * 2**i for i, (d, f) in enumerate(zip(digits, flips))))
    return peers


def kernel(
    n,
    features_ref,
    adjacency_ref,
    first_seen_ref,
    pos_ref,
    w_struct_ref,
    w_query_ref,
    w_key_ref,
    w_value_ref,
    w_out_ref,
    w_up_ref,
    w_down_ref,
    gain_ref,
    out_ref,
    hidden,
    adjacent,
    conv,
    arrived,
    finished,
    ws,
    wqkv,
    wo,
    wu,
    wd,
    pos,
    qkv,
    heads_out,
    bias,
    inner,
    in_sems,
    first_sems,
    link_sems,
    go_send,
    go_recv,
    back_send,
    back_recv,
    out_sem,
):
    me = lax.axis_index("snap")
    blocks = ws.shape[0]
    _, local, _, owned, width = hidden.shape
    steps = pos.shape[0]
    nodes = n * owned
    chunks = owned // CHUNK
    head_dim = width // HEADS
    rows = steps * GROUP
    groups = CHUNK // GROUP

    def load_links(c):
        part = pl.ds(c * CHUNK, CHUNK)
        return pltpu.make_async_copy(
            adjacency_ref.at[:, :, part], adjacent.at[:, :, part], link_sems.at[c]
        )

    moves = [
        (w_struct_ref, ws),
        (w_query_ref, wqkv.at[:, :, pl.ds(0, width)]),
        (w_key_ref, wqkv.at[:, :, pl.ds(width, width)]),
        (w_value_ref, wqkv.at[:, :, pl.ds(2 * width, width)]),
        (w_out_ref, wo),
        (w_up_ref, wu),
        (w_down_ref, wd),
    ]
    loads = [
        pltpu.make_async_copy(src, dst, in_sems.at[i]) for i, (src, dst) in enumerate(moves)
    ]
    first = pl.ds(0, CHUNK)
    first_loads = [
        (
            pltpu.make_async_copy(features_ref.at[s], hidden.at[0, s], first_sems.at[s, 0]),
            pltpu.make_async_copy(
                adjacency_ref.at[s, :, first], adjacent.at[s, :, first], first_sems.at[s, 1]
            ),
        )
        for s in range(local)
    ]
    for s, pair in enumerate(first_loads):
        for load in pair:
            load.start()
        if s == 0:
            loads[0].start()
    for c in range(1, chunks):
        load_links(c).start()
    for load in loads[1:]:
        load.start()

    barrier = pltpu.get_barrier_semaphore()
    for k in range(1, n):
        pl.semaphore_signal(
            barrier,
            inc=1,
            device_id={"snap": lax.rem(me + k, n)},
            device_id_type=pl.DeviceIdType.MESH,
        )
    pos[...] = jnp.broadcast_to(
        pos_ref[...].astype(F32)[:, None, :], (steps, GROUP, width)
    )

    def send(src, dst, send_sem, recv_sem, peer):
        return pltpu.make_async_remote_copy(
            src_ref=src,
            dst_ref=dst,
            send_sem=send_sem,
            recv_sem=recv_sem,
            device_id={"snap": peer},
            device_id_type=pl.DeviceIdType.MESH,
        )

    others = pl.ds(0, n - 1)

    def go(b, c, peer):
        return send(
            conv.at[b, c, peer],
            arrived.at[b, c, pl.ds(me * local, local)],
            go_send.at[b],
            go_recv.at[b, c],
            peer,
        )

    def back(b, c, peer, target):
        return send(
            finished.at[b, c, pl.ds(peer * local, local)],
            target.at[:, me, pl.ds(c * CHUNK, CHUNK)],
            back_send.at[b],
            back_recv.at[b, local],
            peer,
        )

    def go_one(b, s, peer):
        return send(
            conv.at[b, 0, peer, pl.ds(s, 1)],
            arrived.at[b, 0, pl.ds(me * local + s, 1)],
            go_send.at[b],
            go_recv.at[b, 0],
            peer,
        )

    def back_one(b, s, peer, target):
        return send(
            finished.at[b, chunks - 1, pl.ds(peer * local + s, 1)],
            target.at[pl.ds(s, 1), me, pl.ds((chunks - 1) * CHUNK, CHUNK)],
            back_send.at[b],
            back_recv.at[b, s],
            peer,
        )

    def await_chunk(b, c):
        view = arrived.at[b, c, pl.ds(0, (n - 1) * local)]
        send(view, view, go_send.at[b], go_recv.at[b, c], me).wait_recv()

    def await_early(b, target):
        if chunks > 1:
            view = target.at[:, others, pl.ds(0, (chunks - 1) * CHUNK)]
            send(view, view, back_send.at[b], back_recv.at[b, local], me).wait_recv()

    def await_late(b, s, target):
        view = target.at[pl.ds(s, 1), others, pl.ds((chunks - 1) * CHUNK, CHUNK)]
        send(view, view, back_send.at[b], back_recv.at[b, s], me).wait_recv()

    def await_sent(b):
        view = conv.at[b, :, others]
        send(view, view, go_send.at[b], go_recv.at[b, 0], me).wait_send()
        view = finished.at[b, :, pl.ds(0, (n - 1) * local)]
        send(view, view, back_send.at[b], back_recv.at[b, 0], me).wait_send()

    def convolve(b, c, snapshots):
        mine = pl.ds(c * CHUNK, CHUNK)
        blended, own_rows = [], []
        for s in snapshots:
            links = adjacent[s, :, mine, :].reshape(n * CHUNK, nodes).astype(F32)
            degree = 1.0 + jnp.sum(links, axis=-1, keepdims=True)
            own = hidden[b, s, :, mine, :].reshape(n * CHUNK, width).astype(F32)
            summed = matmul(links.astype(BF16), hidden[b, s].reshape(nodes, width)) + own
            blended.append((summed * (1.0 / degree)).astype(BF16))
            own_rows.append(own)
        projected = matmul(jnp.concatenate(blended, axis=0), ws[b])
        projected = jnp.where(projected > 0, projected, jnp.exp(jnp.minimum(projected, 0.0)) - 1.0)
        result = (projected + jnp.concatenate(own_rows, axis=0)).astype(BF16)
        result = result.reshape(len(snapshots), n, CHUNK, width)
        for i, s in enumerate(snapshots):
            conv[b, c, :, s] = result[i]

    def mask_of(c, g):
        lane = lax.broadcasted_iota(jnp.int32, (1, rows), 1)
        seen = jnp.zeros((1, rows), jnp.int32)
        for i in range(GROUP):
            seen = jnp.where(
                lane % GROUP == i, first_seen_ref[c * CHUNK + g * GROUP + i], seen
            )
        row_at = lax.broadcasted_iota(jnp.int32, (rows, rows), 0)
        col_at = lax.broadcasted_iota(jnp.int32, (rows, rows), 1)
        t, j = row_at // GROUP, col_at // GROUP
        allowed = (row_at % GROUP == col_at % GROUP) & (j <= t) & ((j >= seen) | (j == t))
        bias[g] = jnp.where(allowed, 0.0, -1e30)

    def attend(g, tile):
        at = g * rows
        span = rows // SPANS
        tile_lane = lax.broadcasted_iota(jnp.int32, (1, LANES), 1)
        q = qkv[at : at + rows, tile * LANES : (tile + 1) * LANES]
        k = qkv[at : at + rows, width + tile * LANES : width + (tile + 1) * LANES]
        v = qkv[at : at + rows, 2 * width + tile * LANES : 2 * width + (tile + 1) * LANES]
        totals = [None] * SPANS
        for h in range(LANES // head_dim):
            chosen = jnp.where(tile_lane // head_dim == h, 1.0, 0.0).astype(BF16)
            keys = k * chosen
            wide = jnp.concatenate(
                [v * chosen, jnp.broadcast_to(chosen, (rows, LANES))], axis=1
            )
            for i in range(SPANS):
                start, end = i * span, (i + 1) * span
                scores = lax.dot_general(
                    q[start:end],
                    keys[:end],
                    (((1,), (1,)), ((), ())),
                    preferred_element_type=F32,
                )
                scores = scores + bias[g, start:end, :end]
                top = jnp.max(scores, axis=-1, keepdims=True)
                weights = jnp.exp(scores - top).astype(BF16)
                part = matmul(weights, wide[:end])
                totals[i] = part if h == 0 else totals[i] + part
        for i, total in enumerate(totals):
            heads_out[
                at + i * span : at + (i + 1) * span, tile * LANES : (tile + 1) * LANES
            ] = (total[:, :LANES] / total[:, LANES:]).astype(BF16)

    def group_steps(b, c, g, results):
        at = slice(g * rows, (g + 1) * rows)
        arrivals = arrived[b, c].astype(F32)[:, g * GROUP : (g + 1) * GROUP, :]
        summed = (arrivals + pos[...]).reshape(rows, width)
        normed = layer_norm(summed, gain_ref[b, pl.ds(0, 1), :]).astype(BF16)
        mask_of(c, g)
        yield
        qkv[at, :width] = (matmul(normed, wqkv[b, :, :width]) * head_dim ** (-0.5)).astype(BF16)
        yield
        qkv[at, width : 2 * width] = matmul(normed, wqkv[b, :, width : 2 * width]).astype(BF16)
        yield
        qkv[at, 2 * width :] = matmul(normed, wqkv[b, :, 2 * width :]).astype(BF16)
        yield
        for tile in range(width // LANES):
            attend(g, tile)
            yield
        attended = summed + matmul(heads_out[at, :], wo[b])
        normed_two = layer_norm(attended, gain_ref[b, pl.ds(1, 1), :]).astype(BF16)
        yield
        hidden_units = wu.shape[2]
        for start in range(0, hidden_units, FF_TILE):
            part = slice(start, start + FF_TILE)
            inner[at, part] = gelu(matmul(normed_two, wu[b, :, part])).astype(BF16)
            yield
        results[g] = (attended + matmul(inner[at, :], wd[b])).reshape(steps, GROUP, width)

    def temporal(b, c):
        results = [None] * groups
        waiting = [group_steps(b, c, g, results) for g in range(groups)]
        running, tick = [], 0
        while waiting or running:
            if waiting and tick % LAG == 0:
                running.append(waiting.pop(0))
            for steps_left in list(running):
                if next(steps_left, 0) == 0:
                    running.remove(steps_left)
            tick += 1
        finished[b, c] = jnp.concatenate(results, axis=1).astype(BF16)

    last = blocks - 1
    peers = peers_of(me, n)
    own = pl.ds(me * local, local)

    @pl.loop(0, blocks)
    def _(b):
        @pl.when(b > 0)
        def _():
            await_early(b - 1, hidden.at[b])

        for s in range(local):

            @pl.when(b == 0)
            def _():
                for load in first_loads[s]:
                    load.wait()
                if s == 0:
                    loads[0].wait()

            @pl.when(b > 0)
            def _():
                await_late(b - 1, s, hidden.at[b])

            convolve(b, 0, [s])
            if s == 0:

                @pl.when(b == 0)
                def _():
                    pl.semaphore_wait(barrier, n - 1)

            for peer in peers:
                go_one(b, s, peer).start()
        arrived[b, 0, own] = conv[b, 0, me]

        @pl.loop(1, chunks)
        def _(c):
            @pl.when(b == 0)
            def _():
                load_links(c).wait()

            convolve(b, c, range(local))
            for peer in peers:
                go(b, c, peer).start()
            arrived[b, c, own] = conv[b, c, me]

        @pl.when(b == 0)
        def _():
            for load in loads[1:]:
                load.wait()

        @pl.loop(0, chunks)
        def _(c):
            await_chunk(b, c)
            temporal(b, c)
            part = pl.ds(c * CHUNK, CHUNK)

            def send_back(target):
                @pl.when(c < chunks - 1)
                def _():
                    for peer in peers:
                        back(b, c, peer, target).start()

                @pl.when(c == chunks - 1)
                def _():
                    for s in range(local):
                        for peer in peers:
                            back_one(b, s, peer, target).start()

            @pl.when(b < last)
            def _():
                send_back(hidden.at[b + 1])
                hidden[b + 1, :, me, part, :] = finished[b, c, own]

            @pl.when(b == last)
            def _():
                send_back(out_ref)
                pltpu.make_async_copy(
                    finished.at[b, c, own], out_ref.at[:, me, part], out_sem
                ).start()

    for b in range(blocks):
        await_sent(b)
    await_early(last, out_ref)
    for s in range(local):
        await_late(last, s, out_ref)
    pltpu.make_async_copy(
        finished.at[last, :, pl.ds(0, local)], finished.at[last, :, pl.ds(0, local)], out_sem
    ).wait()


def on_device(n, features, adjacency, first_seen, pos_embed, *weights):
    local, nodes, width = features.shape
    blocks, _, hidden_units = weights[5].shape
    owned = nodes // n
    chunks = owned // CHUNK
    steps = pos_embed.shape[0]
    chunk_rows = steps * CHUNK
    anywhere = pl.BlockSpec(memory_space=pl.ANY)
    in_vmem = pl.BlockSpec(memory_space=pltpu.VMEM)
    result = pl.pallas_call(
        functools.partial(kernel, n),
        out_shape=jax.ShapeDtypeStruct((local, n, owned, width), BF16),
        in_specs=[
            anywhere,
            anywhere,
            pl.BlockSpec(memory_space=pltpu.SMEM),
            in_vmem,
            *[anywhere] * 7,
            in_vmem,
        ],
        out_specs=anywhere,
        scratch_shapes=[
            pltpu.VMEM((blocks, local, n, owned, width), BF16),
            pltpu.VMEM((local, n, owned, nodes), jnp.int32),
            pltpu.VMEM((blocks, chunks, n, local, CHUNK, width), BF16),
            pltpu.VMEM((blocks, chunks, steps, CHUNK, width), BF16),
            pltpu.VMEM((blocks, chunks, steps, CHUNK, width), BF16),
            pltpu.VMEM((blocks, width, width), BF16),
            pltpu.VMEM((blocks, width, 3 * width), BF16),
            pltpu.VMEM((blocks, width, width), BF16),
            pltpu.VMEM((blocks, width, hidden_units), BF16),
            pltpu.VMEM((blocks, hidden_units, width), BF16),
            pltpu.VMEM((steps, GROUP, width), F32),
            pltpu.VMEM((chunk_rows, 3 * width), BF16),
            pltpu.VMEM((chunk_rows, width), BF16),
            pltpu.VMEM((CHUNK // GROUP, steps * GROUP, steps * GROUP), F32),
            pltpu.VMEM((chunk_rows, hidden_units), BF16),
            pltpu.SemaphoreType.DMA((7,)),
            pltpu.SemaphoreType.DMA((local, 2)),
            pltpu.SemaphoreType.DMA((chunks,)),
            pltpu.SemaphoreType.DMA((blocks,)),
            pltpu.SemaphoreType.DMA((blocks, chunks)),
            pltpu.SemaphoreType.DMA((blocks,)),
            pltpu.SemaphoreType.DMA((blocks, local + 1)),
            pltpu.SemaphoreType.DMA,
        ],
        compiler_params=pltpu.CompilerParams(
            collective_id=0, has_side_effects=True, vmem_limit_bytes=56 * 2**20
        ),
    )(
        features.reshape(local, n, owned, width),
        adjacency.reshape(local, n, owned, nodes),
        first_seen,
        pos_embed,
        *weights,
    )
    return result.reshape(local, nodes, width)


def solution(mesh):
    in_specs = (
        P("snap", "clus", None),
        P("snap", "clus", None),
        P(("clus", "snap")),
        *[P()] * 9,
    )
    return jax.shard_map(
        functools.partial(on_device, mesh.shape["snap"]),
        mesh=mesh,
        in_specs=in_specs,
        out_specs=P("snap", "clus", None),
        check_vma=False,
    )
```

```python
import functools

import jax
import jax.numpy as jnp
from jax import lax
from jax.experimental import pallas as pl
from jax.experimental.pallas import tpu as pltpu
from jax.sharding import PartitionSpec as P

HEADS = 8
LANES = 128
CHUNK = 16
GROUP = 8
SPANS = 2
LAG = 4
FF_TILE = 256
F32 = jnp.float32
BF16 = jnp.bfloat16


def layer_norm(values_in, gain):
    average = jnp.mean(values_in, axis=-1, keepdims=True)
    centred = values_in - average
    scattered_rows = jnp.mean(centred * centred, axis=-1, keepdims=True)
    return centred * lax.rsqrt(scattered_rows + 1e-05) * gain


def matmul(left, right):
    return jnp.dot(left, right, preferred_element_type=F32)


def gelu(x):
    half = 0.5 * x
    return half + half * jnp.tanh(x * (0.7978845608028654 + 0.035677408136300125 * (x * x)))


def peers_of(me, n):
    bits = n.bit_length() - 1
    if 2**bits != n or bits < 3:
        return [lax.rem(me + k, n) for k in range(1, n)]
    digits = [(me // 2**i) % 2 for i in range(bits)]
    core = digits[0]
    order = sorted(range(1, n), key=lambda m: (m < 2, bin(m // 2).count("1"), m))
    peers = []
    for m in order:
        flips = [(m // 2**i) % 2 for i in range(bits)]
        low, high = flips[1], flips[2]
        flips[1] = low * (1 - core) + high * core
        flips[2] = high * (1 - core) + low * core
        peers.append(sum(((d + f) % 2) * 2**i for i, (d, f) in enumerate(zip(digits, flips))))
    return peers


def kernel(
    n,
    features_ref,
    adjacency_ref,
    first_seen_ref,
    pos_ref,
    w_struct_ref,
    w_query_ref,
    w_key_ref,
    w_value_ref,
    w_out_ref,
    w_up_ref,
    w_down_ref,
    gain_ref,
    out_ref,
    hidden,
    adjacent,
    conv,
    arrived,
    finished,
    ws,
    wqkv,
    wo,
    wu,
    wd,
    pos,
    qkv,
    heads_out,
    bias,
    inner,
    in_sems,
    first_sems,
    link_sems,
    go_send,
    go_recv,
    back_send,
    back_recv,
    out_sem,
):
    me = lax.axis_index("snap")
    blocks = ws.shape[0]
    _, local, _, owned, width = hidden.shape
    steps = pos.shape[0]
    nodes = n * owned
    chunks = owned // CHUNK
    head_dim = width // HEADS
    rows = steps * GROUP
    groups = CHUNK // GROUP

    def load_links(c):
        part = pl.ds(c * CHUNK, CHUNK)
        return pltpu.make_async_copy(
            adjacency_ref.at[:, :, part], adjacent.at[:, :, part], link_sems.at[c]
        )

    moves = [
        (w_struct_ref, ws),
        (w_query_ref, wqkv.at[:, :, pl.ds(0, width)]),
        (w_key_ref, wqkv.at[:, :, pl.ds(width, width)]),
        (w_value_ref, wqkv.at[:, :, pl.ds(2 * width, width)]),
        (w_out_ref, wo),
        (w_up_ref, wu),
        (w_down_ref, wd),
    ]
    loads = [
        pltpu.make_async_copy(src, dst, in_sems.at[i]) for i, (src, dst) in enumerate(moves)
    ]
    first = pl.ds(0, CHUNK)
    first_loads = [
        (
            pltpu.make_async_copy(features_ref.at[s], hidden.at[0, s], first_sems.at[s, 0]),
            pltpu.make_async_copy(
                adjacency_ref.at[s, :, first], adjacent.at[s, :, first], first_sems.at[s, 1]
            ),
        )
        for s in range(local)
    ]
    for s, pair in enumerate(first_loads):
        for load in pair:
            load.start()
        if s == 0:
            loads[0].start()
    for c in range(1, chunks):
        load_links(c).start()
    for load in loads[1:]:
        load.start()

    barrier = pltpu.get_barrier_semaphore()
    for k in range(1, n):
        pl.semaphore_signal(
            barrier,
            inc=1,
            device_id={"snap": lax.rem(me + k, n)},
            device_id_type=pl.DeviceIdType.MESH,
        )
    pos[...] = jnp.broadcast_to(
        pos_ref[...].astype(F32)[:, None, :], (steps, GROUP, width)
    )

    def send(src, dst, send_sem, recv_sem, peer):
        return pltpu.make_async_remote_copy(
            src_ref=src,
            dst_ref=dst,
            send_sem=send_sem,
            recv_sem=recv_sem,
            device_id={"snap": peer},
            device_id_type=pl.DeviceIdType.MESH,
        )

    others = pl.ds(0, n - 1)

    def go(b, c, peer):
        return send(
            conv.at[b, c, peer],
            arrived.at[b, c, pl.ds(me * local, local)],
            go_send.at[b],
            go_recv.at[b, c],
            peer,
        )

    def back(b, c, peer, target):
        return send(
            finished.at[b, c, pl.ds(peer * local, local)],
            target.at[:, me, pl.ds(c * CHUNK, CHUNK)],
            back_send.at[b],
            back_recv.at[b, local],
            peer,
        )

    def go_one(b, s, peer):
        return send(
            conv.at[b, 0, peer, pl.ds(s, 1)],
            arrived.at[b, 0, pl.ds(me * local + s, 1)],
            go_send.at[b],
            go_recv.at[b, 0],
            peer,
        )

    def back_one(b, s, peer, target):
        return send(
            finished.at[b, chunks - 1, pl.ds(peer * local + s, 1)],
            target.at[pl.ds(s, 1), me, pl.ds((chunks - 1) * CHUNK, CHUNK)],
            back_send.at[b],
            back_recv.at[b, s],
            peer,
        )

    def await_chunk(b, c):
        view = arrived.at[b, c, pl.ds(0, (n - 1) * local)]
        send(view, view, go_send.at[b], go_recv.at[b, c], me).wait_recv()

    def await_early(b, target):
        if chunks > 1:
            view = target.at[:, others, pl.ds(0, (chunks - 1) * CHUNK)]
            send(view, view, back_send.at[b], back_recv.at[b, local], me).wait_recv()

    def await_late(b, s, target):
        view = target.at[pl.ds(s, 1), others, pl.ds((chunks - 1) * CHUNK, CHUNK)]
        send(view, view, back_send.at[b], back_recv.at[b, s], me).wait_recv()

    def await_sent(b):
        view = conv.at[b, :, others]
        send(view, view, go_send.at[b], go_recv.at[b, 0], me).wait_send()
        view = finished.at[b, :, pl.ds(0, (n - 1) * local)]
        send(view, view, back_send.at[b], back_recv.at[b, 0], me).wait_send()

    def convolve(b, c, snapshots):
        mine = pl.ds(c * CHUNK, CHUNK)
        blended, own_rows = [], []
        for s in snapshots:
            links = adjacent[s, :, mine, :].reshape(n * CHUNK, nodes).astype(F32)
            degree = 1.0 + jnp.sum(links, axis=-1, keepdims=True)
            own = hidden[b, s, :, mine, :].reshape(n * CHUNK, width).astype(F32)
            summed = matmul(links.astype(BF16), hidden[b, s].reshape(nodes, width)) + own
            blended.append((summed * (1.0 / degree)).astype(BF16))
            own_rows.append(own)
        projected = matmul(jnp.concatenate(blended, axis=0), ws[b])
        projected = jnp.where(projected > 0, projected, jnp.exp(jnp.minimum(projected, 0.0)) - 1.0)
        result = (projected + jnp.concatenate(own_rows, axis=0)).astype(BF16)
        result = result.reshape(len(snapshots), n, CHUNK, width)
        for i, s in enumerate(snapshots):
            conv[b, c, :, s] = result[i]

    def mask_of(c, g):
        lane = lax.broadcasted_iota(jnp.int32, (1, rows), 1)
        seen = jnp.zeros((1, rows), jnp.int32)
        for i in range(GROUP):
            seen = jnp.where(
                lane % GROUP == i, first_seen_ref[c * CHUNK + g * GROUP + i], seen
            )
        row_at = lax.broadcasted_iota(jnp.int32, (rows, rows), 0)
        col_at = lax.broadcasted_iota(jnp.int32, (rows, rows), 1)
        t, j = row_at // GROUP, col_at // GROUP
        allowed = (row_at % GROUP == col_at % GROUP) & (j <= t) & ((j >= seen) | (j == t))
        bias[g] = jnp.where(allowed, 0.0, -1e30)

    def attend(g, tile):
        at = g * rows
        span = rows // SPANS
        tile_lane = lax.broadcasted_iota(jnp.int32, (1, LANES), 1)
        q = qkv[at : at + rows, tile * LANES : (tile + 1) * LANES]
        k = qkv[at : at + rows, width + tile * LANES : width + (tile + 1) * LANES]
        v = qkv[at : at + rows, 2 * width + tile * LANES : 2 * width + (tile + 1) * LANES]
        totals = [None] * SPANS
        for h in range(LANES // head_dim):
            chosen = jnp.where(tile_lane // head_dim == h, 1.0, 0.0).astype(BF16)
            keys = k * chosen
            wide = jnp.concatenate(
                [v * chosen, jnp.broadcast_to(chosen, (rows, LANES))], axis=1
            )
            for i in range(SPANS):
                start, end = i * span, (i + 1) * span
                scores = lax.dot_general(
                    q[start:end],
                    keys[:end],
                    (((1,), (1,)), ((), ())),
                    preferred_element_type=F32,
                )
                scores = scores + bias[g, start:end, :end]
                top = jnp.max(scores, axis=-1, keepdims=True)
                weights = jnp.exp(scores - top).astype(BF16)
                part = matmul(weights, wide[:end])
                totals[i] = part if h == 0 else totals[i] + part
        for i, total in enumerate(totals):
            heads_out[
                at + i * span : at + (i + 1) * span, tile * LANES : (tile + 1) * LANES
            ] = (total[:, :LANES] / total[:, LANES:]).astype(BF16)

    def group_steps(b, c, g, results):
        at = slice(g * rows, (g + 1) * rows)
        arrivals = arrived[b, c].astype(F32)[:, g * GROUP : (g + 1) * GROUP, :]
        summed = (arrivals + pos[...]).reshape(rows, width)
        normed = layer_norm(summed, gain_ref[b, pl.ds(0, 1), :]).astype(BF16)
        mask_of(c, g)
        yield
        qkv[at, :width] = (matmul(normed, wqkv[b, :, :width]) * head_dim ** (-0.5)).astype(BF16)
        yield
        qkv[at, width : 2 * width] = matmul(normed, wqkv[b, :, width : 2 * width]).astype(BF16)
        yield
        qkv[at, 2 * width :] = matmul(normed, wqkv[b, :, 2 * width :]).astype(BF16)
        yield
        for tile in range(width // LANES):
            attend(g, tile)
            yield
        attended = summed + matmul(heads_out[at, :], wo[b])
        normed_two = layer_norm(attended, gain_ref[b, pl.ds(1, 1), :]).astype(BF16)
        yield
        hidden_units = wu.shape[2]
        for start in range(0, hidden_units, FF_TILE):
            part = slice(start, start + FF_TILE)
            inner[at, part] = gelu(matmul(normed_two, wu[b, :, part])).astype(BF16)
            yield
        results[g] = (attended + matmul(inner[at, :], wd[b])).reshape(steps, GROUP, width)

    def temporal(b, c):
        results = [None] * groups
        waiting = [group_steps(b, c, g, results) for g in range(groups)]
        running, tick = [], 0
        while waiting or running:
            if waiting and tick % LAG == 0:
                running.append(waiting.pop(0))
            for steps_left in list(running):
                if next(steps_left, 0) == 0:
                    running.remove(steps_left)
            tick += 1
        finished[b, c] = jnp.concatenate(results, axis=1).astype(BF16)

    last = blocks - 1
    peers = peers_of(me, n)
    own = pl.ds(me * local, local)

    @pl.loop(0, blocks)
    def _(b):
        @pl.when(b > 0)
        def _():
            await_early(b - 1, hidden.at[b])

        for s in range(local):

            @pl.when(b == 0)
            def _():
                for load in first_loads[s]:
                    load.wait()
                if s == 0:
                    loads[0].wait()

            @pl.when(b > 0)
            def _():
                await_late(b - 1, s, hidden.at[b])

            convolve(b, 0, [s])
            if s == 0:

                @pl.when(b == 0)
                def _():
                    pl.semaphore_wait(barrier, n - 1)

            for peer in peers:
                go_one(b, s, peer).start()
        arrived[b, 0, own] = conv[b, 0, me]

        @pl.loop(1, chunks)
        def _(c):
            @pl.when(b == 0)
            def _():
                load_links(c).wait()

            convolve(b, c, range(local))
            for peer in peers:
                go(b, c, peer).start()
            arrived[b, c, own] = conv[b, c, me]

        @pl.when(b == 0)
        def _():
            for load in loads[1:]:
                load.wait()

        @pl.loop(0, chunks)
        def _(c):
            await_chunk(b, c)
            temporal(b, c)
            part = pl.ds(c * CHUNK, CHUNK)

            def send_back(target):
                @pl.when(c < chunks - 1)
                def _():
                    for peer in peers:
                        back(b, c, peer, target).start()

                @pl.when(c == chunks - 1)
                def _():
                    for s in range(local):
                        for peer in peers:
                            back_one(b, s, peer, target).start()

            @pl.when(b < last)
            def _():
                send_back(hidden.at[b + 1])
                hidden[b + 1, :, me, part, :] = finished[b, c, own]

            @pl.when(b == last)
            def _():
                send_back(out_ref)
                pltpu.make_async_copy(
                    finished.at[b, c, own], out_ref.at[:, me, part], out_sem
                ).start()

    for b in range(blocks):
        await_sent(b)
    await_early(last, out_ref)
    for s in range(local):
        await_late(last, s, out_ref)
    pltpu.make_async_copy(
        finished.at[last, :, pl.ds(0, local)], finished.at[last, :, pl.ds(0, local)], out_sem
    ).wait()


def hand_over(rows_ref, out_ref, sem):
    local, n = rows_ref.shape[:2]
    cuts = (0, n // 2, n)
    for s in range(local):
        for start, end in zip(cuts, cuts[1:]):
            part = pl.ds(start, end - start)
            pltpu.make_async_copy(rows_ref.at[s, part], out_ref.at[s, part], sem).start()
    pltpu.make_async_copy(rows_ref, out_ref, sem).wait()


def on_device(n, features, adjacency, first_seen, pos_embed, *weights):
    local, nodes, width = features.shape
    blocks, _, hidden_units = weights[5].shape
    owned = nodes // n
    chunks = owned // CHUNK
    steps = pos_embed.shape[0]
    chunk_rows = steps * CHUNK
    anywhere = pl.BlockSpec(memory_space=pl.ANY)
    in_vmem = pl.BlockSpec(memory_space=pltpu.VMEM)
    result = pl.pallas_call(
        functools.partial(kernel, n),
        out_shape=jax.ShapeDtypeStruct((local, n, owned, width), BF16),
        in_specs=[
            anywhere,
            anywhere,
            pl.BlockSpec(memory_space=pltpu.SMEM),
            in_vmem,
            *[anywhere] * 7,
            in_vmem,
        ],
        out_specs=anywhere,
        scratch_shapes=[
            pltpu.VMEM((blocks, local, n, owned, width), BF16),
            pltpu.VMEM((local, n, owned, nodes), jnp.int32),
            pltpu.VMEM((blocks, chunks, n, local, CHUNK, width), BF16),
            pltpu.VMEM((blocks, chunks, steps, CHUNK, width), BF16),
            pltpu.VMEM((blocks, chunks, steps, CHUNK, width), BF16),
            pltpu.VMEM((blocks, width, width), BF16),
            pltpu.VMEM((blocks, width, 3 * width), BF16),
            pltpu.VMEM((blocks, width, width), BF16),
            pltpu.VMEM((blocks, width, hidden_units), BF16),
            pltpu.VMEM((blocks, hidden_units, width), BF16),
            pltpu.VMEM((steps, GROUP, width), F32),
            pltpu.VMEM((chunk_rows, 3 * width), BF16),
            pltpu.VMEM((chunk_rows, width), BF16),
            pltpu.VMEM((CHUNK // GROUP, steps * GROUP, steps * GROUP), F32),
            pltpu.VMEM((chunk_rows, hidden_units), BF16),
            pltpu.SemaphoreType.DMA((7,)),
            pltpu.SemaphoreType.DMA((local, 2)),
            pltpu.SemaphoreType.DMA((chunks,)),
            pltpu.SemaphoreType.DMA((blocks,)),
            pltpu.SemaphoreType.DMA((blocks, chunks)),
            pltpu.SemaphoreType.DMA((blocks,)),
            pltpu.SemaphoreType.DMA((blocks, local + 1)),
            pltpu.SemaphoreType.DMA,
        ],
        compiler_params=pltpu.CompilerParams(
            collective_id=0, has_side_effects=True, vmem_limit_bytes=56 * 2**20
        ),
    )(
        features.reshape(local, n, owned, width),
        adjacency.reshape(local, n, owned, nodes),
        first_seen,
        pos_embed,
        *weights,
    )
    result = pl.pallas_call(
        hand_over,
        out_shape=jax.ShapeDtypeStruct(result.shape, BF16),
        in_specs=[anywhere],
        out_specs=anywhere,
        scratch_shapes=[pltpu.SemaphoreType.DMA],
        compiler_params=pltpu.CompilerParams(vmem_limit_bytes=56 * 2**20),
    )(result)
    return result.reshape(local, nodes, width)


def solution(mesh):
    in_specs = (
        P("snap", "clus", None),
        P("snap", "clus", None),
        P(("clus", "snap")),
        *[P()] * 9,
    )
    return jax.shard_map(
        functools.partial(on_device, mesh.shape["snap"]),
        mesh=mesh,
        in_specs=in_specs,
        out_specs=P("snap", "clus", None),
        check_vma=False,
    )
```
